32 devices in a mesh: replica: 2 (over y), tensor: 4 (over z), adapter: 4 (over x, core).
Axes of the slice: x: 2, y: 2, z: 4, core: 2. Of those that a mesh axis runs over, the one named last changes fastest.
Arguments:
- requests: bfloat16 [3072, 8192], P(('replica', 'adapter'), 'tensor'), parts along dimension 0, may hold values from -6 to 6
- query_weight: bfloat16 [8192, 8192], P(None, 'tensor'), may hold values from -0.0625 to 0.0625
- adapter_down_factor: bfloat16 [32, 64, 8192], P('adapter', None, 'tensor'), may hold values from -0.0625 to 0.0625
- adapter_up_factor: bfloat16 [32, 64, 8192], P('adapter', None, 'tensor'), may hold values from -0.75 to 0.75
- request_adapter_index: int32 [3072, 1], P(('replica', 'adapter')), parts along dimension 0, may hold values from 0 to 31; in each aligned block of 384 rows (0 to 383, 384 to 767, ...) at most 24 rows name the same one
Outputs:
- queries: bfloat16 [3072, 8192], P(('replica', 'adapter'), 'tensor'), parts along dimension 0
The draws below stay inside these ranges and needn't reach their ends.
There are 2 independent parts, one for each index of `replica`. The reference program is written for one: setup_inputs(seed, part) draws one part's arguments, and reference() takes and returns one part's arrays. A program takes and returns all parts, laid end to end along the dimension named above; an argument that names none is the same for every part. Nothing has to cross between parts.
Inputs may be any that keep to these rules, and one draw needn't show every extreme that they name: `request_adapter_index`: among the 384 requests of one device (aligned blocks of rows), no adapter is named more than 24 times.
All inputs are finite; a program needn't handle non-finite values.
Results may differ from the reference program's by a relative error of at most 0.0075.
Values may be sent and summed in bfloat16 or wider, within the bound.
No kernel may reach another device: no remote copies, remote signals or barrier semaphores. Data moves between devices by JAX's collectives and lax.ppermute only.
A program may use at most 128 MiB of HBM per device.

```python
import math
import jax
import jax.numpy as jnp
import numpy as np
from jax import lax

MODEL_WIDTH = 8192
ADAPTER_RANK = 64
R_DEV = 384
REQUESTS = 1536
ADAPTER_COUNT = 32
CAP = 24


def block_scale(own_key, extent, pieces, low, high):
    level = 1.0
    for position, parts in pieces:
        heights = jax.random.uniform(jax.random.fold_in(jax.random.fold_in(own_key, 6), position), (parts,), jnp.float32, low / len(pieces), high / len(pieces))
        level = level * jnp.repeat(jnp.exp(heights), extent[position] // parts).reshape((-1,) + (1,) * (len(extent) - 1 - position))
    return level


def routed_block(stream_key, own, number, rows, count, top, limit, skew):
    ranking = jax.random.permutation(stream_key, count)
    crowded, usual = portions_of(count, rows * top, limit, skew, True), portions_of(count, rows * top, limit, skew, False)
    places = jnp.arange(count)

    def named(sizes, turn):
        used = int((sizes > 0).sum())
        fixed = max(1, used // 4)
        moved = fixed + (places - fixed + turn * (used - fixed)) % max(1, count - fixed)
        return jnp.zeros((count,), jnp.int32).at[ranking[jnp.where(places < fixed, places, moved)]].set(jnp.asarray(sizes, jnp.int32))

    sizes = jnp.where(number % 4 == 0, named(crowded, number // 4), named(usual, number - number // 4 - 1))
    mixed = jax.random.permutation(jax.random.fold_in(own, 3), count)
    donor, receiver = mixed[0:count // 2 * 2:2], mixed[1:count // 2 * 2:2]
    slack = jnp.minimum(sizes[donor] - 1, limit - sizes[receiver]) // 2
    slack = jnp.where((donor == ranking[0]) | (receiver == ranking[0]) | (sizes[receiver] == 0), 0, jnp.maximum(slack, 0))
    moved = jax.random.randint(jax.random.fold_in(own, 4), (count // 2,), 0, 1 << 20) % (slack + 1)
    sizes = sizes.at[donor].add(-moved).at[receiver].add(moved)
    members = jnp.searchsorted(jnp.cumsum(sizes), jnp.arange(rows * top), side="right").astype(jnp.int32)
    table = members.reshape(top, rows).T
    table = table[jax.random.permutation(jax.random.fold_in(own, 1), rows)]
    turn = jax.random.randint(jax.random.fold_in(own, 2), (rows, 1), 0, top)
    return jnp.take_along_axis(table, (jnp.arange(top)[None, :] + turn) % top, axis=1)


def portions_of(number_of, total, most, skew, full):
    portions = [(1 << 20) // math.isqrt(grade ** skew) + 1 for grade in range(1, number_of + 1)]
    largest = most if full else min(most, max(-(-total // number_of), total * portions[0] // sum(portions)))
    least = 1 if total - largest >= number_of - 1 else 0
    counts, spare = [largest] + [least] * (number_of - 1), total - largest - least * (number_of - 1)
    while spare > 0:
        candidates = [i for i in range(1, number_of) if counts[i] < largest] or [i for i in range(1, number_of) if counts[i] < most]
        pool, left = sum([portions[i] for i in candidates]), spare
        for i in candidates:
            addition = min(most - counts[i], max(1, left * portions[i] // pool), spare)
            counts[i] = counts[i] + addition
            spare = spare - addition
    return np.array(counts)


def normal_values(own_key, extent, scale, reach, pieces=(), kind=jnp.bfloat16):
    factor_of = block_scale(own_key, extent, pieces, -0.22, 0.18) if pieces else 1.0
    entries = jax.random.normal(own_key, extent, jnp.float32) * scale * factor_of
    return jnp.minimum(jnp.maximum(entries, -reach), reach).astype(kind)


def setup_inputs(seed: int = 0, part: int = 0) -> dict:
    keys = jax.random.split(jax.random.key(seed), 6)
    part_keys = jax.random.split(jax.random.fold_in(keys[5], part), 6)
    requests = normal_values(part_keys[0], (REQUESTS, MODEL_WIDTH), 1.0, 6.0, ((0, 4), (1, 4)))
    query_weight = normal_values(keys[1], (MODEL_WIDTH, MODEL_WIDTH), MODEL_WIDTH ** -0.5, 0.0625, ((1, 4),))
    adapter_down_factor = normal_values(keys[2], (ADAPTER_COUNT, ADAPTER_RANK, MODEL_WIDTH), MODEL_WIDTH ** -0.5, 0.0625, ((0, 4), (2, 4)))
    adapter_up_factor = normal_values(keys[3], (ADAPTER_COUNT, ADAPTER_RANK, MODEL_WIDTH), ADAPTER_RANK ** -0.5, 0.75, ((0, 4), (2, 4)))
    request_adapter_index_keys = jax.random.split(jax.random.fold_in(part_keys[4], 1), REQUESTS // R_DEV)
    request_adapter_index_turns = jax.random.permutation(jax.random.fold_in(part_keys[4], 3), REQUESTS // R_DEV)
    request_adapter_index = jax.vmap(lambda own, number: routed_block(jax.random.fold_in(part_keys[4], 2), own, number, R_DEV, ADAPTER_COUNT, 1, CAP, 2))(request_adapter_index_keys, request_adapter_index_turns).reshape((REQUESTS, 1))
    return dict(requests=requests, query_weight=query_weight, adapter_down_factor=adapter_down_factor, adapter_up_factor=adapter_up_factor, request_adapter_index=request_adapter_index)


adapter_scale = 0.5


def reference(requests, query_weight, adapter_down_factor, adapter_up_factor, request_adapter_index):
    base_query_output = jnp.dot(requests, query_weight, preferred_element_type=jnp.float32)
    block_size = math.gcd(REQUESTS, 32)
    blocks = REQUESTS // block_size
    row_blocks = requests.reshape(blocks, block_size, MODEL_WIDTH)
    id_blocks = request_adapter_index[:, 0].reshape(blocks, block_size)

    def one_block(packed):
        block_rows, block_index_list = packed
        down_factor_rows = adapter_down_factor[block_index_list].astype(jnp.float32)
        reduced = jnp.einsum("rd,rkd->rk", block_rows.astype(jnp.float32), down_factor_rows,
                             precision=lax.Precision.HIGHEST).astype(jnp.bfloat16)
        up_factor_rows = adapter_up_factor[block_index_list].astype(jnp.float32)
        lifted = jnp.einsum("rk,rkc->rc", reduced.astype(jnp.float32), up_factor_rows,
                            precision=lax.Precision.HIGHEST)
        return lifted.astype(jnp.bfloat16)

    adapter_corrections = lax.map(one_block, (row_blocks, id_blocks)).reshape(REQUESTS, MODEL_WIDTH)
    return (base_query_output + adapter_scale * adapter_corrections.astype(jnp.float32)).astype(jnp.bfloat16)
```

```python
import jax
import jax.numpy as jnp
from jax import lax
from jax.sharding import PartitionSpec as P

adapter_scale = 0.5
CHUNKS = 2


def rank_spread(count, rank):
    rows = lax.broadcasted_iota(jnp.int32, (count * rank, rank), 0)
    cols = lax.broadcasted_iota(jnp.int32, (count * rank, rank), 1)
    return (rows % rank == cols).astype(jnp.bfloat16)


def owner_mask(adapter_of, first, count, rank):
    cols = lax.broadcasted_iota(jnp.int32, (1, count * rank), 1) // rank + first
    return adapter_of == cols


def gathered_factor(factor, order):
    resident, rank, width = factor.shape
    groups = lax.axis_size("adapter")
    me = lax.axis_index("adapter")
    flat = factor.reshape(resident * rank, width)
    copies = lax.axis_size("replica")
    if groups != 4 or copies != 2:
        whole = lax.all_gather(flat, "adapter", axis=0, tiled=True)
        return [(whole, jnp.int32(0))]
    half = resident * rank // 2
    mine = lax.axis_index("replica")
    across = [(0, 2), (2, 0), (1, 3), (3, 1)]
    beside = [(0, 1), (1, 0), (2, 3), (3, 2)]
    sent = lax.dynamic_slice_in_dim(flat, mine * half, half, 0)
    far_mine = lax.ppermute(sent, "adapter", across)
    far_other = lax.ppermute(far_mine, "replica", [(0, 1), (1, 0)])
    near = lax.ppermute(flat, "adapter", beside)
    near_mine = lax.ppermute(far_mine, "adapter", beside)
    near_other = lax.ppermute(far_other, "adapter", beside)
    h = resident // 2
    return [
        (flat, me * resident),
        (near, (me ^ 1) * resident),
        (far_mine, (me ^ 2) * resident + mine * h),
        (near_mine, (me ^ 3) * resident + mine * h),
        (far_other, (me ^ 2) * resident + (1 - mine) * h),
        (near_other, (me ^ 3) * resident + (1 - mine) * h),
    ]


def local(requests, query_weight, adapter_down_factor, adapter_up_factor, request_adapter_index):
    features = requests.shape[1]
    rank = adapter_down_factor.shape[1]
    spans = lax.axis_size("tensor")
    z = lax.axis_index("tensor")

    def base(block, owner, chunk, width):
        rows = lax.dynamic_slice_in_dim(query_weight, owner * features + chunk * width, width, 0)
        return jnp.dot(block, rows, preferred_element_type=jnp.float32)

    down = gathered_factor(adapter_down_factor, 0)
    up = gathered_factor(adapter_up_factor, 1)

    low = 0.0
    for piece, first in down:
        count = piece.shape[0] // rank
        full = lax.dot_general(
            requests, piece, (((1,), (1,)), ((), ())), preferred_element_type=jnp.float32
        )
        kept = jnp.where(owner_mask(request_adapter_index, first, count, rank), full, 0.0)
        low += jnp.dot(
            kept.astype(jnp.bfloat16), rank_spread(count, rank), preferred_element_type=jnp.float32
        )
    low = low.astype(jnp.bfloat16)

    if spans == 4:
        total = low.astype(jnp.float32)
        for bit in (1, 2, 3):
            total += lax.ppermute(low, "tensor", [(i, i ^ bit) for i in range(4)]).astype(
                jnp.float32
            )
        low = total.astype(jnp.bfloat16)
        width = features // CHUNKS
        pair = [(0, 1), (1, 0), (2, 3), (3, 2)]
        middle = [(1, 2), (2, 1)]
        outward = [(1, 0), (2, 3)]
        inner = (z == 1) | (z == 2)
        acc = base(requests, z, 0, features)
        for c in range(CHUNKS):
            x = requests[:, c * width : (c + 1) * width]
            a1 = lax.ppermute(x, "tensor", pair)
            m1 = lax.ppermute(x, "tensor", middle)
            m2 = lax.ppermute(a1, "tensor", middle)
            e2 = lax.ppermute(m1, "tensor", outward)
            e3 = lax.ppermute(m2, "tensor", outward)
            acc += base(a1, z ^ 1, c, width)
            acc += base(jnp.where(inner, m1, e2), jnp.where(inner, z ^ 3, z ^ 2), c, width)
            acc += base(jnp.where(inner, m2, e3), jnp.where(inner, z ^ 2, z ^ 3), c, width)
    else:
        low = lax.psum(low, "tensor")
        acc = jnp.dot(
            lax.all_gather(requests, "tensor", axis=1, tiled=True),
            query_weight,
            preferred_element_type=jnp.float32,
        )

    for piece, first in up:
        count = piece.shape[0] // rank
        spread = lax.dot_general(
            low * jnp.bfloat16(adapter_scale),
            rank_spread(count, rank),
            (((1,), (1,)), ((), ())),
            preferred_element_type=jnp.float32,
        ).astype(jnp.bfloat16)
        kept = jnp.where(owner_mask(request_adapter_index, first, count, rank), spread, 0)
        acc += jnp.dot(kept, piece, preferred_element_type=jnp.float32)
    return acc.astype(jnp.bfloat16)


def solution(mesh):
    placed = (
        P(("replica", "adapter"), "tensor"),
        P(None, "tensor"),
        P("adapter", None, "tensor"),
        P("adapter", None, "tensor"),
        P(("replica", "adapter"), None),
    )
    return jax.shard_map(
        local,
        mesh=mesh,
        in_specs=placed,
        out_specs=P(("replica", "adapter"), "tensor"),
        check_vma=False,
    )
```

```python
import functools

import jax
import jax.numpy as jnp
from jax import lax
from jax.experimental import pallas as pl
from jax.experimental.pallas import tpu as pltpu
from jax.sharding import PartitionSpec as P

adapter_scale = 0.5
TILE = 512
TINY = 0.2
SHRINK = 0.2
FIRST = 0.2
def cost(rows, depth, cols, SHARE):
    return pl.CostEstimate(
        flops=1 + int(SHARE * 2 * rows * depth * cols),
        bytes_accessed=int(SHARE * (2 * depth * cols + 8 * rows * cols)),
        transcendentals=0,
    )


PARAMS = pltpu.CompilerParams(vmem_limit_bytes=28 * 2**20)


def rank_spread(count, rank):
    rows = lax.broadcasted_iota(jnp.int32, (count * rank, rank), 0)
    cols = lax.broadcasted_iota(jnp.int32, (count * rank, rank), 1)
    return (rows % rank == cols).astype(jnp.bfloat16)


def owner_mask(adapter_of, first, count, rank):
    cols = lax.broadcasted_iota(jnp.int32, (1, count * rank), 1) // rank + first
    return adapter_of == cols


def block_kernel(sizes, row_block, *refs):
    count = sum(sizes)
    xs, weight_ref, out_ref = refs[:count], refs[count], refs[-1]
    value = refs[count + 1][...] if len(refs) > count + 2 else 0.0
    at = i = 0
    for size in sizes:
        x = xs[i][...]
        for other in xs[i + 1 : i + size]:
            x += other[...]
        value += jnp.dot(
            x, weight_ref[at : at + x.shape[1], :], preferred_element_type=jnp.float32
        )
        at += x.shape[1]
        i += size
    out_ref[...] = value.astype(out_ref.dtype)


def add_block(acc, groups, weight, row_block, dtype=jnp.float32, share=TINY):
    rows = groups[0][0].shape[0]
    xs = [x for group in groups for x in group]
    depth = sum(group[0].shape[1] for group in groups)
    cols = weight.shape[1]
    specs = [pl.BlockSpec(x.shape, lambda n, b: (0, 0)) for x in xs]
    specs.append(pl.BlockSpec((depth, TILE), lambda n, b: (b[0], n)))
    tiles = pl.BlockSpec((rows, TILE), lambda n, b: (0, n))
    args = [row_block.astype(jnp.int32).reshape(1), *xs, weight]
    if acc is not None:
        specs.append(tiles)
        args.append(acc)
    return pl.pallas_call(
        functools.partial(block_kernel, tuple(len(group) for group in groups)),
        grid_spec=pltpu.PrefetchScalarGridSpec(
            num_scalar_prefetch=1, grid=(cols // TILE,), in_specs=specs, out_specs=tiles
        ),
        out_shape=jax.ShapeDtypeStruct((rows, cols), dtype),
        compiler_params=PARAMS,
        cost_estimate=cost(rows, depth, cols, share),
    )(*args)


def expand_kernel(counts, rank, firsts, low_ref, owner_ref, acc_ref, *rest):
    pieces, out_ref, spread_ref = rest[: len(counts)], rest[-2], rest[-1]

    @pl.when(pl.program_id(0) == 0)
    def _():
        at = 0
        for i, count in enumerate(counts):
            wide = lax.dot_general(
                low_ref[...],
                rank_spread(count, rank),
                (((1,), (1,)), ((), ())),
                preferred_element_type=jnp.float32,
            )
            kept = jnp.where(owner_mask(owner_ref[...], firsts[i], count, rank), wide, 0.0)
            spread_ref[:, at : at + count * rank] = kept.astype(jnp.bfloat16)
            at += count * rank

    total, at = 0.0, 0
    for i, count in enumerate(counts):
        total += jnp.dot(
            spread_ref[:, at : at + count * rank],
            pieces[i][...],
            preferred_element_type=jnp.float32,
        )
        at += count * rank
    out_ref[...] = acc_ref[...] + adapter_scale * total


def add_expanded(acc, low, owners, up, share=TINY):
    rows, cols = acc.shape
    rank = low.shape[1]
    counts = tuple(piece.shape[0] // rank for piece, _ in up)
    depth = sum(counts) * rank
    tiles = pl.BlockSpec((rows, TILE), lambda n, f: (0, n))
    return pl.pallas_call(
        functools.partial(expand_kernel, counts, rank),
        grid_spec=pltpu.PrefetchScalarGridSpec(
            num_scalar_prefetch=1,
            grid=(cols // TILE,),
            in_specs=[
                pl.BlockSpec((rows, rank), lambda n, f: (0, 0)),
                pl.BlockSpec((rows, 1), lambda n, f: (0, 0)),
                tiles,
            ]
            + [pl.BlockSpec((c * rank, TILE), lambda n, f: (0, n)) for c in counts],
            out_specs=tiles,
            scratch_shapes=[pltpu.VMEM((rows, depth), jnp.bfloat16)],
        ),
        out_shape=jax.ShapeDtypeStruct((rows, cols), jnp.float32),
        compiler_params=PARAMS,
        cost_estimate=cost(rows, depth, cols, share),
    )(jnp.stack([first for _, first in up]).astype(jnp.int32), low, owners, acc, *[p for p, _ in up])


ACROSS = [(0, 2), (2, 0), (1, 3), (3, 1)]
SWAP = [(0, 1), (1, 0)]
BESIDE = [(0, 1), (1, 0), (2, 3), (3, 2)]


def half_of(rows, which):
    half = rows.shape[0] // 2
    return lax.dynamic_slice_in_dim(rows, which * half, half, 0)


def shrink_kernel(count, rank, first, *refs):
    piece, xs, owners = refs[0], refs[1:3], refs[3:5]
    before, outs = refs[5:-2], refs[-2:]
    for i in range(2):
        full = lax.dot_general(
            xs[i][...], piece[...], (((1,), (1,)), ((), ())), preferred_element_type=jnp.float32
        )
        kept = jnp.where(owner_mask(owners[i][...], first[0], count, rank), full, 0.0)
        total = jnp.dot(
            kept.astype(jnp.bfloat16), rank_spread(count, rank), preferred_element_type=jnp.float32
        )
        outs[i][...] = total + before[i][...] if before else total


def add_shrunk(lows, piece, first, xs, owners, rank):
    rows, features = xs[0].shape
    whole = pl.BlockSpec(memory_space=pltpu.VMEM)
    args = [piece, *xs, *owners, *lows]
    return pl.pallas_call(
        functools.partial(shrink_kernel, piece.shape[0] // rank, rank),
        in_specs=[pl.BlockSpec(memory_space=pltpu.SMEM)] + [whole] * len(args),
        out_specs=[whole] * 2,
        out_shape=[jax.ShapeDtypeStruct((rows, rank), jnp.float32)] * 2,
        compiler_params=PARAMS,
        cost_estimate=cost(2 * rows, features, piece.shape[0], SHRINK),
    )(first.astype(jnp.int32).reshape(1), *args)


def local_line(requests, query_weight, adapter_down_factor, adapter_up_factor, owners):
    features = requests.shape[1]
    rank = adapter_down_factor.shape[1]
    z = lax.axis_index("tensor")
    inner = (z == 1) | (z == 2)

    me = lax.axis_index("adapter")
    replica = lax.axis_index("replica")
    resident = adapter_down_factor.shape[0]
    down = adapter_down_factor.reshape(resident * rank, features)
    up = adapter_up_factor.reshape(resident * rank, -1)

    pair, middle, outward = [(0, 1), (1, 0), (2, 3), (3, 2)], [(1, 2), (2, 1)], [(1, 0), (2, 3)]
    second, third = jnp.where(inner, z ^ 3, z ^ 2), jnp.where(inner, z ^ 2, z ^ 3)
    halves = [me * resident, (me ^ 2) * resident + replica * (resident // 2)]
    halves.append((me ^ 2) * resident + (1 - replica) * (resident // 2))

    a1 = lax.ppermute(requests, "tensor", pair)
    m1 = lax.ppermute(requests, "tensor", middle)
    acc = add_block(None, [[requests]], query_weight, z, share=FIRST)
    xs = (requests, lax.ppermute(requests, "adapter", BESIDE))
    both = (owners, lax.ppermute(owners, "adapter", BESIDE))
    down_mine = lax.ppermute(half_of(down, replica), "adapter", ACROSS)
    up_mine = lax.ppermute(half_of(up, replica), "adapter", ACROSS)
    lows = add_shrunk((), down, halves[0], xs, both, rank)
    down_mine, acc, lows = lax.optimization_barrier((down_mine, acc, lows))
    down_other = lax.ppermute(down_mine, "replica", SWAP)
    lows = add_shrunk(lows, down_mine, halves[1], xs, both, rank)
    a1, m1, lows = lax.optimization_barrier((a1, m1, lows))
    m2 = lax.ppermute(a1, "tensor", middle)
    e2 = lax.ppermute(m1, "tensor", outward)
    acc = add_block(acc, [[a1]], query_weight, z ^ 1)
    lows, acc = lax.optimization_barrier((lows, acc))
    lows = add_shrunk(lows, down_other, halves[2], xs, both, rank)
    low = lows[0] + lax.ppermute(lows[1].astype(jnp.bfloat16), "adapter", BESIDE).astype(jnp.float32)
    for bit in (1, 2):
        low = low.astype(jnp.bfloat16)
        low = low.astype(jnp.float32) + lax.ppermute(
            low, "tensor", [(i, i ^ bit) for i in range(4)]
        ).astype(jnp.float32)
    low = low.astype(jnp.bfloat16)
    m2, e2, low = lax.optimization_barrier((m2, e2, low))
    e3 = lax.ppermute(m2, "tensor", outward)

    up_other = lax.ppermute(up_mine, "replica", SWAP)
    up_other, _ = lax.optimization_barrier((up_other, m2))
    near = [lax.ppermute(piece, "adapter", BESIDE) for piece in (up, up_mine, up_other)]
    across = resident - 2 * (me % 2) * resident
    ups = list(zip((up, up_mine, up_other), halves)) + list(zip(near, [h + across for h in halves]))

    acc = add_block(acc, [[m1, e2]], query_weight, second)
    acc = add_expanded(acc, low, owners, ups)
    return add_block(acc, [[m2, e3]], query_weight, third, jnp.bfloat16)


def local_any(requests, query_weight, adapter_down_factor, adapter_up_factor, owners):
    rank, width = adapter_down_factor.shape[1:]
    down, up = (
        lax.all_gather(f, "adapter", axis=0, tiled=True).reshape(-1, width)
        for f in (adapter_down_factor, adapter_up_factor)
    )
    count = down.shape[0] // rank
    full = lax.dot_general(
        requests, down, (((1,), (1,)), ((), ())), preferred_element_type=jnp.float32
    )
    kept = jnp.where(owner_mask(owners, 0, count, rank), full, 0.0).astype(jnp.bfloat16)
    low = jnp.dot(kept, rank_spread(count, rank), preferred_element_type=jnp.float32)
    low = lax.psum(low.astype(jnp.bfloat16), "tensor")
    spread = lax.dot_general(
        low, rank_spread(count, rank), (((1,), (1,)), ((), ())), preferred_element_type=jnp.float32
    )
    kept = jnp.where(owner_mask(owners, 0, count, rank), spread, 0.0).astype(jnp.bfloat16)
    base = jnp.dot(
        lax.all_gather(requests, "tensor", axis=1, tiled=True),
        query_weight,
        preferred_element_type=jnp.float32,
    )
    delta = jnp.dot(kept, up, preferred_element_type=jnp.float32)
    return (base + adapter_scale * delta).astype(jnp.bfloat16)


def solution(mesh):
    placed = (
        P(("replica", "adapter"), "tensor"),
        P(None, "tensor"),
        P("adapter", None, "tensor"),
        P("adapter", None, "tensor"),
        P(("replica", "adapter"), None),
    )
    sizes = tuple(mesh.shape[axis] for axis in ("replica", "tensor", "adapter"))
    return jax.shard_map(
        local_line if sizes == (2, 4, 4) else local_any,
        mesh=mesh,
        in_specs=placed,
        out_specs=P(("replica", "adapter"), "tensor"),
        check_vma=False,
    )
```

```python
import functools

import jax
import jax.numpy as jnp
from jax import lax
from jax.experimental import pallas as pl
from jax.experimental.pallas import tpu as pltpu
from jax.sharding import PartitionSpec as P

adapter_scale = 0.5
TILE = 512
PIECES = 4
TINY = 0.2
SHRINK = 0.2
FIRST = 0.2
def cost(rows, depth, cols, SHARE):
    return pl.CostEstimate(
        flops=1 + int(SHARE * 2 * rows * depth * cols),
        bytes_accessed=int(SHARE * (2 * depth * cols + 8 * rows * cols)),
        transcendentals=0,
    )


PARAMS = pltpu.CompilerParams(vmem_limit_bytes=28 * 2**20)


def rank_spread(count, rank):
    rows = lax.broadcasted_iota(jnp.int32, (count * rank, rank), 0)
    cols = lax.broadcasted_iota(jnp.int32, (count * rank, rank), 1)
    return (rows % rank == cols).astype(jnp.bfloat16)


def owner_mask(adapter_of, first, count, rank):
    cols = lax.broadcasted_iota(jnp.int32, (1, count * rank), 1) // rank + first
    return adapter_of == cols


def block_kernel(sizes, row_block, *refs):
    count = sum(sizes)
    xs, weight_ref, out_ref = refs[:count], refs[count], refs[-1]
    value = refs[count + 1][...] if len(refs) > count + 2 else 0.0
    at = i = 0
    for size in sizes:
        x = xs[i][...]
        for other in xs[i + 1 : i + size]:
            x += other[...]
        value += jnp.dot(
            x, weight_ref[at : at + x.shape[1], :], preferred_element_type=jnp.float32
        )
        at += x.shape[1]
        i += size
    out_ref[...] = value.astype(out_ref.dtype)


def add_block(acc, groups, weight, row_block, dtype=jnp.float32, share=TINY):
    rows = groups[0][0].shape[0]
    xs = [x for group in groups for x in group]
    depth = sum(group[0].shape[1] for group in groups)
    cols = weight.shape[1]
    specs = [pl.BlockSpec(x.shape, lambda n, b: (0, 0)) for x in xs]
    specs.append(pl.BlockSpec((depth, TILE), lambda n, b: (b[0], n)))
    tiles = pl.BlockSpec((rows, TILE), lambda n, b: (0, n))
    args = [row_block.astype(jnp.int32).reshape(1), *xs, weight]
    if acc is not None:
        specs.append(tiles)
        args.append(acc)
    return pl.pallas_call(
        functools.partial(block_kernel, tuple(len(group) for group in groups)),
        grid_spec=pltpu.PrefetchScalarGridSpec(
            num_scalar_prefetch=1, grid=(cols // TILE,), in_specs=specs, out_specs=tiles
        ),
        out_shape=jax.ShapeDtypeStruct((rows, cols), dtype),
        compiler_params=PARAMS,
        cost_estimate=cost(rows, depth, cols, share),
    )(*args)


def last_kernel(inner, here, there, weight_ref, acc_ref, out, x_ref, tiles_ref, came, went):
    depth, cols = weight_ref.shape
    step = depth // PIECES
    pieces = [pl.ds(i * step, step) for i in range(PIECES)]
    wide = cols // PIECES
    spans = [pl.ds(i * wide, wide) for i in range(PIECES)]

    def arriving(source, i):
        return pltpu.make_async_copy(source.at[:, pieces[i]], x_ref.at[:, pieces[i]], came.at[i])

    for source, chosen in ((here, inner[0] == 1), (there, inner[0] == 0)):

        @pl.when(chosen)
        def _(source=source):
            for i in range(PIECES):
                arriving(source, i).start()

    leaving = []
    for n, span in enumerate(spans):
        total = acc_ref[:, span]
        for i, piece in enumerate(pieces):
            if n == 0:
                arriving(there, i).wait()
            total += jnp.dot(
                x_ref[:, piece], weight_ref[piece, span], preferred_element_type=jnp.float32
            )
        tiles_ref[:, span] = total.astype(tiles_ref.dtype)
        leaving.append(pltpu.make_async_copy(tiles_ref.at[:, span], out.at[:, span], went.at[n]))
        leaving[-1].start()
    for copy in leaving:
        copy.wait()


def add_last(acc, inner, here, there, weight):
    rows, depth = here.shape
    cols = weight.shape[1]
    anywhere, resident = pl.BlockSpec(memory_space=pl.ANY), pl.BlockSpec(memory_space=pltpu.VMEM)
    return pl.pallas_call(
        last_kernel,
        in_specs=[pl.BlockSpec(memory_space=pltpu.SMEM), anywhere, anywhere, resident, resident],
        out_specs=anywhere,
        out_shape=jax.ShapeDtypeStruct((rows, cols), jnp.bfloat16),
        scratch_shapes=[
            pltpu.VMEM((rows, depth), jnp.bfloat16),
            pltpu.VMEM((rows, cols), jnp.bfloat16),
            pltpu.SemaphoreType.DMA((PIECES,)),
            pltpu.SemaphoreType.DMA((PIECES,)),
        ],
        compiler_params=pltpu.CompilerParams(vmem_limit_bytes=30 * 2**20),
        cost_estimate=cost(rows, depth, cols, TINY),
    )(inner.astype(jnp.int32).reshape(1), here, there, weight, acc)


def expand_kernel(counts, rank, firsts, low_ref, owner_ref, acc_ref, *rest):
    pieces, out_ref, spread_ref = rest[: len(counts)], rest[-2], rest[-1]

    @pl.when(pl.program_id(0) == 0)
    def _():
        at = 0
        for i, count in enumerate(counts):
            wide = lax.dot_general(
                low_ref[...],
                rank_spread(count, rank),
                (((1,), (1,)), ((), ())),
                preferred_element_type=jnp.float32,
            )
            kept = jnp.where(owner_mask(owner_ref[...], firsts[i], count, rank), wide, 0.0)
            spread_ref[:, at : at + count * rank] = kept.astype(jnp.bfloat16)
            at += count * rank

    total, at = 0.0, 0
    for i, count in enumerate(counts):
        total += jnp.dot(
            spread_ref[:, at : at + count * rank],
            pieces[i][...],
            preferred_element_type=jnp.float32,
        )
        at += count * rank
    out_ref[...] = acc_ref[...] + adapter_scale * total


def add_expanded(acc, low, owners, up, share=TINY):
    rows, cols = acc.shape
    rank = low.shape[1]
    counts = tuple(piece.shape[0] // rank for piece, _ in up)
    depth = sum(counts) * rank
    tiles = pl.BlockSpec((rows, TILE), lambda n, f: (0, n))
    return pl.pallas_call(
        functools.partial(expand_kernel, counts, rank),
        grid_spec=pltpu.PrefetchScalarGridSpec(
            num_scalar_prefetch=1,
            grid=(cols // TILE,),
            in_specs=[
                pl.BlockSpec((rows, rank), lambda n, f: (0, 0)),
                pl.BlockSpec((rows, 1), lambda n, f: (0, 0)),
                tiles,
            ]
            + [pl.BlockSpec((c * rank, TILE), lambda n, f: (0, n)) for c in counts],
            out_specs=tiles,
            scratch_shapes=[pltpu.VMEM((rows, depth), jnp.bfloat16)],
        ),
        out_shape=jax.ShapeDtypeStruct((rows, cols), jnp.float32),
        compiler_params=PARAMS,
        cost_estimate=cost(rows, depth, cols, share),
    )(jnp.stack([first for _, first in up]).astype(jnp.int32), low, owners, acc, *[p for p, _ in up])


ACROSS = [(0, 2), (2, 0), (1, 3), (3, 1)]
SWAP = [(0, 1), (1, 0)]
BESIDE = [(0, 1), (1, 0), (2, 3), (3, 2)]


def half_of(rows, which):
    half = rows.shape[0] // 2
    return lax.dynamic_slice_in_dim(rows, which * half, half, 0)


def shrink_kernel(count, rank, first, *refs):
    piece, xs, owners = refs[0], refs[1:3], refs[3:5]
    before, outs = refs[5:-2], refs[-2:]
    for i in range(2):
        full = lax.dot_general(
            xs[i][...], piece[...], (((1,), (1,)), ((), ())), preferred_element_type=jnp.float32
        )
        kept = jnp.where(owner_mask(owners[i][...], first[0], count, rank), full, 0.0)
        total = jnp.dot(
            kept.astype(jnp.bfloat16), rank_spread(count, rank), preferred_element_type=jnp.float32
        )
        outs[i][...] = total + before[i][...] if before else total


def add_shrunk(lows, piece, first, xs, owners, rank):
    rows, features = xs[0].shape
    whole = pl.BlockSpec(memory_space=pltpu.VMEM)
    args = [piece, *xs, *owners, *lows]
    return pl.pallas_call(
        functools.partial(shrink_kernel, piece.shape[0] // rank, rank),
        in_specs=[pl.BlockSpec(memory_space=pltpu.SMEM)] + [whole] * len(args),
        out_specs=[whole] * 2,
        out_shape=[jax.ShapeDtypeStruct((rows, rank), jnp.float32)] * 2,
        compiler_params=PARAMS,
        cost_estimate=cost(2 * rows, features, piece.shape[0], SHRINK),
    )(first.astype(jnp.int32).reshape(1), *args)


def local_line(requests, query_weight, adapter_down_factor, adapter_up_factor, owners):
    features = requests.shape[1]
    rank = adapter_down_factor.shape[1]
    z = lax.axis_index("tensor")
    inner = (z == 1) | (z == 2)

    me = lax.axis_index("adapter")
    replica = lax.axis_index("replica")
    resident = adapter_down_factor.shape[0]
    down = adapter_down_factor.reshape(resident * rank, features)
    up = adapter_up_factor.reshape(resident * rank, -1)

    pair, middle, outward = [(0, 1), (1, 0), (2, 3), (3, 2)], [(1, 2), (2, 1)], [(1, 0), (2, 3)]
    second, third = jnp.where(inner, z ^ 3, z ^ 2), jnp.where(inner, z ^ 2, z ^ 3)
    halves = [me * resident, (me ^ 2) * resident + replica * (resident // 2)]
    halves.append((me ^ 2) * resident + (1 - replica) * (resident // 2))

    a1 = lax.ppermute(requests, "tensor", pair)
    m1 = lax.ppermute(requests, "tensor", middle)
    acc = add_block(None, [[requests]], query_weight, z, share=FIRST)
    xs = (requests, lax.ppermute(requests, "adapter", BESIDE))
    both = (owners, lax.ppermute(owners, "adapter", BESIDE))
    down_mine = lax.ppermute(half_of(down, replica), "adapter", ACROSS)
    up_half, up_near = half_of(up, replica), lax.ppermute(up, "adapter", BESIDE)
    lows = add_shrunk((), down, halves[0], xs, both, rank)
    down_mine, acc, lows, up_half, up_near = lax.optimization_barrier(
        (down_mine, acc, lows, up_half, up_near)
    )
    up_mine = lax.ppermute(up_half, "adapter", ACROSS)
    down_other = lax.ppermute(down_mine, "replica", SWAP)
    a1, down_mine = lax.optimization_barrier((a1, down_mine))
    lows = add_shrunk(lows, down_mine, halves[1], xs, both, rank)
    m2 = lax.ppermute(a1, "tensor", middle)
    m1, a1 = lax.optimization_barrier((m1, a1))
    e2 = lax.ppermute(m1, "tensor", outward)
    acc = add_block(acc, [[a1]], query_weight, z ^ 1)
    lows, acc = lax.optimization_barrier((lows, acc))
    lows = add_shrunk(lows, down_other, halves[2], xs, both, rank)
    low = lows[0] + lax.ppermute(lows[1].astype(jnp.bfloat16), "adapter", BESIDE).astype(jnp.float32)
    shares = jnp.broadcast_to(low.astype(jnp.bfloat16)[None], (4, *low.shape))
    shares = lax.all_to_all(shares, "tensor", 0, 0)
    low = jnp.sum(shares.astype(jnp.float32), axis=0).astype(jnp.bfloat16)
    m2, e2, low = lax.optimization_barrier((m2, e2, low))
    e3 = lax.ppermute(m2, "tensor", outward)

    up_other = lax.ppermute(up_mine, "replica", SWAP)
    up_other, _ = lax.optimization_barrier((up_other, m2))
    near = [up_near, *[lax.ppermute(piece, "adapter", BESIDE) for piece in (up_mine, up_other)]]
    across = resident - 2 * (me % 2) * resident
    ups = list(zip((up, up_mine, up_other), halves)) + list(zip(near, [h + across for h in halves]))

    acc = add_block(acc, [[m1, e2]], query_weight, second)
    weight = lax.dynamic_slice_in_dim(query_weight, third * features, features, 0)
    acc, weight = lax.optimization_barrier((acc, weight))
    acc = add_expanded(acc, low, owners, ups)
    return add_last(acc, inner, m2, e3, weight)


def local_any(requests, query_weight, adapter_down_factor, adapter_up_factor, owners):
    rank, width = adapter_down_factor.shape[1:]
    down, up = (
        lax.all_gather(f, "adapter", axis=0, tiled=True).reshape(-1, width)
        for f in (adapter_down_factor, adapter_up_factor)
    )
    count = down.shape[0] // rank
    full = lax.dot_general(
        requests, down, (((1,), (1,)), ((), ())), preferred_element_type=jnp.float32
    )
    kept = jnp.where(owner_mask(owners, 0, count, rank), full, 0.0).astype(jnp.bfloat16)
    low = jnp.dot(kept, rank_spread(count, rank), preferred_element_type=jnp.float32)
    low = lax.psum(low.astype(jnp.bfloat16), "tensor")
    spread = lax.dot_general(
        low, rank_spread(count, rank), (((1,), (1,)), ((), ())), preferred_element_type=jnp.float32
    )
    kept = jnp.where(owner_mask(owners, 0, count, rank), spread, 0.0).astype(jnp.bfloat16)
    base = jnp.dot(
        lax.all_gather(requests, "tensor", axis=1, tiled=True),
        query_weight,
        preferred_element_type=jnp.float32,
    )
    delta = jnp.dot(kept, up, preferred_element_type=jnp.float32)
    return (base + adapter_scale * delta).astype(jnp.bfloat16)


def solution(mesh):
    placed = (
        P(("replica", "adapter"), "tensor"),
        P(None, "tensor"),
        P("adapter", None, "tensor"),
        P("adapter", None, "tensor"),
        P(("replica", "adapter"), None),
    )
    sizes = tuple(mesh.shape[axis] for axis in ("replica", "tensor", "adapter"))
    return jax.shard_map(
        local_line if sizes == (2, 4, 4) else local_any,
        mesh=mesh,
        in_specs=placed,
        out_specs=P(("replica", "adapter"), "tensor"),
        check_vma=False,
    )
```

```python
import functools

import jax
import jax.numpy as jnp
from jax import lax
from jax.experimental import pallas as pl
from jax.experimental.pallas import tpu as pltpu
from jax.sharding import PartitionSpec as P

adapter_scale = 0.5
TILE = 512
PIECES = 4
TINY = 0.2
SHRINK = 0.2
FIRST = 0.2
def cost(rows, depth, cols, SHARE):
    return pl.CostEstimate(
        flops=1 + int(SHARE * 2 * rows * depth * cols),
        bytes_accessed=int(SHARE * (2 * depth * cols + 8 * rows * cols)),
        transcendentals=0,
    )


PARAMS = pltpu.CompilerParams(vmem_limit_bytes=28 * 2**20)


def rank_spread(count, rank):
    rows = lax.broadcasted_iota(jnp.int32, (count * rank, rank), 0)
    cols = lax.broadcasted_iota(jnp.int32, (count * rank, rank), 1)
    return (rows % rank == cols).astype(jnp.bfloat16)


def owner_mask(adapter_of, first, count, rank):
    cols = lax.broadcasted_iota(jnp.int32, (1, count * rank), 1) // rank + first
    return adapter_of == cols


def block_kernel(sizes, flags, *refs):
    count = sum(sizes)
    xs, weight_ref, out_ref = refs[:count], refs[count], refs[-1]
    value = refs[count + 1][...] if len(refs) > count + 2 else 0.0
    at = i = 0
    for size in sizes:
        x = xs[i][...]
        if size == 2:
            x = jnp.where(flags[1] == 1, x, xs[i + 1][...])
        value += jnp.dot(
            x, weight_ref[at : at + x.shape[1], :], preferred_element_type=jnp.float32
        )
        at += x.shape[1]
        i += size
    out_ref[...] = value.astype(out_ref.dtype)


def add_block(acc, groups, weight, row_block, first=0, dtype=jnp.float32, share=TINY):
    rows = groups[0][0].shape[0]
    xs = [x for group in groups for x in group]
    depth = sum(group[0].shape[1] for group in groups)
    cols = weight.shape[1]
    specs = [pl.BlockSpec(x.shape, lambda n, b: (0, 0)) for x in xs]
    specs.append(pl.BlockSpec((depth, TILE), lambda n, b: (b[0], n)))
    tiles = pl.BlockSpec((rows, TILE), lambda n, b: (0, n))
    args = [jnp.stack([row_block, first]).astype(jnp.int32), *xs, weight]
    if acc is not None:
        specs.append(tiles)
        args.append(acc)
    return pl.pallas_call(
        functools.partial(block_kernel, tuple(len(group) for group in groups)),
        grid_spec=pltpu.PrefetchScalarGridSpec(
            num_scalar_prefetch=1, grid=(cols // TILE,), in_specs=specs, out_specs=tiles
        ),
        out_shape=jax.ShapeDtypeStruct((rows, cols), dtype),
        compiler_params=PARAMS,
        cost_estimate=cost(rows, depth, cols, share),
    )(*args)


def last_kernel(inner, here, there, weight_ref, acc_ref, out, x_ref, tiles_ref, came, went):
    depth, cols = weight_ref.shape
    step = depth // PIECES
    pieces = [pl.ds(i * step, step) for i in range(PIECES)]
    wide = cols // PIECES
    spans = [pl.ds(i * wide, wide) for i in range(PIECES)]

    def arriving(source, i):
        return pltpu.make_async_copy(source.at[:, pieces[i]], x_ref.at[:, pieces[i]], came.at[i])

    for source, chosen in ((here, inner[0] == 1), (there, inner[0] == 0)):

        @pl.when(chosen)
        def _(source=source):
            for i in range(PIECES):
                arriving(source, i).start()

    leaving = []
    for n, span in enumerate(spans):
        total = acc_ref[:, span]
        for i, piece in enumerate(pieces):
            if n == 0:
                arriving(there, i).wait()
            total += jnp.dot(
                x_ref[:, piece], weight_ref[piece, span], preferred_element_type=jnp.float32
            )
        tiles_ref[:, span] = total.astype(tiles_ref.dtype)
        leaving.append(pltpu.make_async_copy(tiles_ref.at[:, span], out.at[:, span], went.at[n]))
        leaving[-1].start()
    for copy in leaving:
        copy.wait()


def add_last(acc, inner, here, there, weight):
    rows, depth = here.shape
    cols = weight.shape[1]
    anywhere, resident = pl.BlockSpec(memory_space=pl.ANY), pl.BlockSpec(memory_space=pltpu.VMEM)
    return pl.pallas_call(
        last_kernel,
        in_specs=[pl.BlockSpec(memory_space=pltpu.SMEM), anywhere, anywhere, resident, resident],
        out_specs=anywhere,
        out_shape=jax.ShapeDtypeStruct((rows, cols), jnp.bfloat16),
        scratch_shapes=[
            pltpu.VMEM((rows, depth), jnp.bfloat16),
            pltpu.VMEM((rows, cols), jnp.bfloat16),
            pltpu.SemaphoreType.DMA((PIECES,)),
            pltpu.SemaphoreType.DMA((PIECES,)),
        ],
        compiler_params=pltpu.CompilerParams(vmem_limit_bytes=30 * 2**20),
        cost_estimate=cost(rows, depth, cols, TINY),
    )(inner.astype(jnp.int32).reshape(1), here, there, weight, acc)


def expand_kernel(counts, rank, firsts, low_ref, owner_ref, acc_ref, *rest):
    pieces, out_ref, spread_ref = rest[: len(counts)], rest[-2], rest[-1]

    @pl.when(pl.program_id(0) == 0)
    def _():
        at = 0
        for i, count in enumerate(counts):
            wide = lax.dot_general(
                low_ref[...],
                rank_spread(count, rank),
                (((1,), (1,)), ((), ())),
                preferred_element_type=jnp.float32,
            )
            kept = jnp.where(owner_mask(owner_ref[...], firsts[i], count, rank), wide, 0.0)
            spread_ref[:, at : at + count * rank] = kept.astype(jnp.bfloat16)
            at += count * rank

    total, at = 0.0, 0
    for i, count in enumerate(counts):
        total += jnp.dot(
            spread_ref[:, at : at + count * rank],
            pieces[i][...],
            preferred_element_type=jnp.float32,
        )
        at += count * rank
    out_ref[...] = acc_ref[...] + adapter_scale * total


def add_expanded(acc, low, owners, up, share=TINY):
    rows, cols = acc.shape
    rank = low.shape[1]
    counts = tuple(piece.shape[0] // rank for piece, _ in up)
    depth = sum(counts) * rank
    tiles = pl.BlockSpec((rows, TILE), lambda n, f: (0, n))
    return pl.pallas_call(
        functools.partial(expand_kernel, counts, rank),
        grid_spec=pltpu.PrefetchScalarGridSpec(
            num_scalar_prefetch=1,
            grid=(cols // TILE,),
            in_specs=[
                pl.BlockSpec((rows, rank), lambda n, f: (0, 0)),
                pl.BlockSpec((rows, 1), lambda n, f: (0, 0)),
                tiles,
            ]
            + [pl.BlockSpec((c * rank, TILE), lambda n, f: (0, n)) for c in counts],
            out_specs=tiles,
            scratch_shapes=[pltpu.VMEM((rows, depth), jnp.bfloat16)],
        ),
        out_shape=jax.ShapeDtypeStruct((rows, cols), jnp.float32),
        compiler_params=PARAMS,
        cost_estimate=cost(rows, depth, cols, share),
    )(jnp.stack([first for _, first in up]).astype(jnp.int32), low, owners, acc, *[p for p, _ in up])


ACROSS = [(0, 2), (2, 0), (1, 3), (3, 1)]
SWAP = [(0, 1), (1, 0)]
BESIDE = [(0, 1), (1, 0), (2, 3), (3, 2)]


def half_of(rows, which):
    half = rows.shape[0] // 2
    return lax.dynamic_slice_in_dim(rows, which * half, half, 0)


def shrink_kernel(count, rank, first, *refs):
    piece, xs, owners = refs[0], refs[1:3], refs[3:5]
    before, outs = refs[5:-2], refs[-2:]
    for i in range(2):
        full = lax.dot_general(
            xs[i][...], piece[...], (((1,), (1,)), ((), ())), preferred_element_type=jnp.float32
        )
        kept = jnp.where(owner_mask(owners[i][...], first[0], count, rank), full, 0.0)
        total = jnp.dot(
            kept.astype(jnp.bfloat16), rank_spread(count, rank), preferred_element_type=jnp.float32
        )
        outs[i][...] = total + before[i][...] if before else total


def add_shrunk(lows, piece, first, xs, owners, rank):
    rows, features = xs[0].shape
    whole = pl.BlockSpec(memory_space=pltpu.VMEM)
    args = [piece, *xs, *owners, *lows]
    return pl.pallas_call(
        functools.partial(shrink_kernel, piece.shape[0] // rank, rank),
        in_specs=[pl.BlockSpec(memory_space=pltpu.SMEM)] + [whole] * len(args),
        out_specs=[whole] * 2,
        out_shape=[jax.ShapeDtypeStruct((rows, rank), jnp.float32)] * 2,
        compiler_params=PARAMS,
        cost_estimate=cost(2 * rows, features, piece.shape[0], SHRINK),
    )(first.astype(jnp.int32).reshape(1), *args)


def local_line(requests, query_weight, adapter_down_factor, adapter_up_factor, owners):
    features = requests.shape[1]
    rank = adapter_down_factor.shape[1]
    z = lax.axis_index("tensor")
    inner = (z == 1) | (z == 2)

    me = lax.axis_index("adapter")
    replica = lax.axis_index("replica")
    resident = adapter_down_factor.shape[0]
    down = adapter_down_factor.reshape(resident * rank, features)
    up = adapter_up_factor.reshape(resident * rank, -1)

    pair, middle = [(0, 1), (1, 0), (2, 3), (3, 2)], [(1, 2), (2, 1)]
    second, third = jnp.where(inner, z ^ 3, z ^ 2), jnp.where(inner, z ^ 2, z ^ 3)
    halves = [me * resident, (me ^ 2) * resident + replica * (resident // 2)]
    halves.append((me ^ 2) * resident + (1 - replica) * (resident // 2))

    a1 = lax.ppermute(requests, "tensor", pair)
    m1 = lax.ppermute(requests, "tensor", middle)
    acc = add_block(None, [[requests]], query_weight, z, share=FIRST)
    xs = (requests, lax.ppermute(requests, "adapter", BESIDE))
    both = (owners, lax.ppermute(owners, "adapter", BESIDE))
    down_mine = lax.ppermute(half_of(down, replica), "adapter", ACROSS)
    up_half, up_near = half_of(up, replica), lax.ppermute(up, "adapter", BESIDE)
    lows = add_shrunk((), down, halves[0], xs, both, rank)
    down_mine, acc, lows, up_half, up_near = lax.optimization_barrier(
        (down_mine, acc, lows, up_half, up_near)
    )
    up_mine = lax.ppermute(up_half, "adapter", ACROSS)
    down_other = lax.ppermute(down_mine, "replica", SWAP)
    a1, down_mine = lax.optimization_barrier((a1, down_mine))
    lows = add_shrunk(lows, down_mine, halves[1], xs, both, rank)
    m2 = lax.ppermute(a1, "tensor", middle)
    e2 = lax.ppermute(m1, "tensor", pair)
    acc = add_block(acc, [[a1]], query_weight, z ^ 1)
    lows, acc = lax.optimization_barrier((lows, acc))
    lows = add_shrunk(lows, down_other, halves[2], xs, both, rank)
    low = lows[0] + lax.ppermute(lows[1].astype(jnp.bfloat16), "adapter", BESIDE).astype(jnp.float32)
    shares = jnp.broadcast_to(low.astype(jnp.bfloat16)[None], (4, *low.shape))
    shares = lax.all_to_all(shares, "tensor", 0, 0)
    low = jnp.sum(shares.astype(jnp.float32), axis=0).astype(jnp.bfloat16)
    m2, e2, low = lax.optimization_barrier((m2, e2, low))
    e3 = lax.ppermute(m2, "tensor", pair)

    up_other = lax.ppermute(up_mine, "replica", SWAP)
    up_other, _ = lax.optimization_barrier((up_other, m2))
    near = [up_near, *[lax.ppermute(piece, "adapter", BESIDE) for piece in (up_mine, up_other)]]
    across = resident - 2 * (me % 2) * resident
    ups = list(zip((up, up_mine, up_other), halves)) + list(zip(near, [h + across for h in halves]))

    acc = add_block(acc, [[m1, e2]], query_weight, second, inner.astype(jnp.int32))
    weight = lax.dynamic_slice_in_dim(query_weight, third * features, features, 0)
    acc, weight = lax.optimization_barrier((acc, weight))
    acc = add_expanded(acc, low, owners, ups)
    return add_last(acc, inner, m2, e3, weight)


def local_any(requests, query_weight, adapter_down_factor, adapter_up_factor, owners):
    rank, width = adapter_down_factor.shape[1:]
    down, up = (
        lax.all_gather(f, "adapter", axis=0, tiled=True).reshape(-1, width)
        for f in (adapter_down_factor, adapter_up_factor)
    )
    count = down.shape[0] // rank
    full = lax.dot_general(
        requests, down, (((1,), (1,)), ((), ())), preferred_element_type=jnp.float32
    )
    kept = jnp.where(owner_mask(owners, 0, count, rank), full, 0.0).astype(jnp.bfloat16)
    low = jnp.dot(kept, rank_spread(count, rank), preferred_element_type=jnp.float32)
    low = lax.psum(low.astype(jnp.bfloat16), "tensor")
    spread = lax.dot_general(
        low, rank_spread(count, rank), (((1,), (1,)), ((), ())), preferred_element_type=jnp.float32
    )
    kept = jnp.where(owner_mask(owners, 0, count, rank), spread, 0.0).astype(jnp.bfloat16)
    base = jnp.dot(
        lax.all_gather(requests, "tensor", axis=1, tiled=True),
        query_weight,
        preferred_element_type=jnp.float32,
    )
    delta = jnp.dot(kept, up, preferred_element_type=jnp.float32)
    return (base + adapter_scale * delta).astype(jnp.bfloat16)


def solution(mesh):
    placed = (
        P(("replica", "adapter"), "tensor"),
        P(None, "tensor"),
        P("adapter", None, "tensor"),
        P("adapter", None, "tensor"),
        P(("replica", "adapter"), None),
    )
    sizes = tuple(mesh.shape[axis] for axis in ("replica", "tensor", "adapter"))
    return jax.shard_map(
        local_line if sizes == (2, 4, 4) else local_any,
        mesh=mesh,
        in_specs=placed,
        out_specs=P(("replica", "adapter"), "tensor"),
        check_vma=False,
    )
```

```python
import functools

import jax
import jax.numpy as jnp
from jax import lax
from jax.experimental import pallas as pl
from jax.experimental.pallas import tpu as pltpu
from jax.sharding import PartitionSpec as P

adapter_scale = 0.5
TILE = 512
PIECES = 4
TINY = 0.2
SHRINK = 0.2
FIRST = 0.2
def cost(rows, depth, cols, SHARE):
    return pl.CostEstimate(
        flops=1 + int(SHARE * 2 * rows * depth * cols),
        bytes_accessed=int(SHARE * (2 * depth * cols + 8 * rows * cols)),
        transcendentals=0,
    )


PARAMS = pltpu.CompilerParams(vmem_limit_bytes=28 * 2**20)


def rank_spread(count, rank):
    rows = lax.broadcasted_iota(jnp.int32, (count * rank, rank), 0)
    cols = lax.broadcasted_iota(jnp.int32, (count * rank, rank), 1)
    return (rows % rank == cols).astype(jnp.bfloat16)


def owner_mask(adapter_of, first, count, rank):
    cols = lax.broadcasted_iota(jnp.int32, (1, count * rank), 1) // rank + first
    return adapter_of == cols


def block_kernel(sizes, flags, *refs):
    count = sum(sizes)
    xs, weight_ref, out_ref = refs[:count], refs[count], refs[-1]
    value = refs[count + 1][...] if len(refs) > count + 2 else 0.0
    at = i = 0
    for size in sizes:
        x = xs[i][...]
        if size == 2:
            x = jnp.where(flags[1] == 1, x, xs[i + 1][...])
        value += jnp.dot(
            x, weight_ref[at : at + x.shape[1], :], preferred_element_type=jnp.float32
        )
        at += x.shape[1]
        i += size
    out_ref[...] = value.astype(out_ref.dtype)


def add_block(acc, groups, weight, row_block, first=0, dtype=jnp.float32, share=TINY):
    rows = groups[0][0].shape[0]
    xs = [x for group in groups for x in group]
    depth = sum(group[0].shape[1] for group in groups)
    cols = weight.shape[1]
    specs = [pl.BlockSpec(x.shape, lambda n, b: (0, 0)) for x in xs]
    specs.append(pl.BlockSpec((depth, TILE), lambda n, b: (b[0], n)))
    tiles = pl.BlockSpec((rows, TILE), lambda n, b: (0, n))
    args = [jnp.stack([row_block, first]).astype(jnp.int32), *xs, weight]
    if acc is not None:
        specs.append(tiles)
        args.append(acc)
    return pl.pallas_call(
        functools.partial(block_kernel, tuple(len(group) for group in groups)),
        grid_spec=pltpu.PrefetchScalarGridSpec(
            num_scalar_prefetch=1, grid=(cols // TILE,), in_specs=specs, out_specs=tiles
        ),
        out_shape=jax.ShapeDtypeStruct((rows, cols), dtype),
        compiler_params=PARAMS,
        cost_estimate=cost(rows, depth, cols, share),
    )(*args)


def last_kernel(inner, here, there, weight_ref, acc_ref, out, x_ref, tiles_ref, came, went):
    depth, cols = weight_ref.shape
    step = depth // PIECES
    pieces = [pl.ds(i * step, step) for i in range(PIECES)]
    wide = cols // PIECES
    spans = [pl.ds(i * wide, wide) for i in range(PIECES)]

    def arriving(source, i):
        return pltpu.make_async_copy(source.at[:, pieces[i]], x_ref.at[:, pieces[i]], came.at[i])

    for source, chosen in ((here, inner[0] == 1), (there, inner[0] == 0)):

        @pl.when(chosen)
        def _(source=source):
            for i in range(PIECES):
                arriving(source, i).start()

    leaving = []
    for n, span in enumerate(spans):
        total = acc_ref[:, span]
        for i, piece in enumerate(pieces):
            if n == 0:
                arriving(there, i).wait()
            total += jnp.dot(
                x_ref[:, piece], weight_ref[piece, span], preferred_element_type=jnp.float32
            )
        tiles_ref[:, span] = total.astype(tiles_ref.dtype)
        leaving.append(pltpu.make_async_copy(tiles_ref.at[:, span], out.at[:, span], went.at[n]))
        leaving[-1].start()
    for copy in leaving:
        copy.wait()


def add_last(acc, inner, here, there, weight):
    rows, depth = here.shape
    cols = weight.shape[1]
    anywhere, resident = pl.BlockSpec(memory_space=pl.ANY), pl.BlockSpec(memory_space=pltpu.VMEM)
    return pl.pallas_call(
        last_kernel,
        in_specs=[pl.BlockSpec(memory_space=pltpu.SMEM), anywhere, anywhere, resident, resident],
        out_specs=anywhere,
        out_shape=jax.ShapeDtypeStruct((rows, cols), jnp.bfloat16),
        scratch_shapes=[
            pltpu.VMEM((rows, depth), jnp.bfloat16),
            pltpu.VMEM((rows, cols), jnp.bfloat16),
            pltpu.SemaphoreType.DMA((PIECES,)),
            pltpu.SemaphoreType.DMA((PIECES,)),
        ],
        compiler_params=pltpu.CompilerParams(vmem_limit_bytes=30 * 2**20),
        cost_estimate=cost(rows, depth, cols, TINY),
    )(inner.astype(jnp.int32).reshape(1), here, there, weight, acc)


def expand_kernel(counts, rank, firsts, low_ref, owner_ref, acc_ref, *rest):
    pieces, out_ref, spread_ref = rest[: len(counts)], rest[-2], rest[-1]

    @pl.when(pl.program_id(0) == 0)
    def _():
        at = 0
        for i, count in enumerate(counts):
            wide = lax.dot_general(
                low_ref[...],
                rank_spread(count, rank),
                (((1,), (1,)), ((), ())),
                preferred_element_type=jnp.float32,
            )
            kept = jnp.where(owner_mask(owner_ref[...], firsts[i], count, rank), wide, 0.0)
            spread_ref[:, at : at + count * rank] = kept.astype(jnp.bfloat16)
            at += count * rank

    total, at = 0.0, 0
    for i, count in enumerate(counts):
        total += jnp.dot(
            spread_ref[:, at : at + count * rank],
            pieces[i][...],
            preferred_element_type=jnp.float32,
        )
        at += count * rank
    out_ref[...] = acc_ref[...] + adapter_scale * total


def add_expanded(acc, low, owners, up, share=TINY):
    rows, cols = acc.shape
    rank = low.shape[1]
    counts = tuple(piece.shape[0] // rank for piece, _ in up)
    depth = sum(counts) * rank
    tiles = pl.BlockSpec((rows, TILE), lambda n, f: (0, n))
    return pl.pallas_call(
        functools.partial(expand_kernel, counts, rank),
        grid_spec=pltpu.PrefetchScalarGridSpec(
            num_scalar_prefetch=1,
            grid=(cols // TILE,),
            in_specs=[
                pl.BlockSpec((rows, rank), lambda n, f: (0, 0)),
                pl.BlockSpec((rows, 1), lambda n, f: (0, 0)),
                tiles,
            ]
            + [pl.BlockSpec((c * rank, TILE), lambda n, f: (0, n)) for c in counts],
            out_specs=tiles,
            scratch_shapes=[pltpu.VMEM((rows, depth), jnp.bfloat16)],
        ),
        out_shape=jax.ShapeDtypeStruct((rows, cols), jnp.float32),
        compiler_params=PARAMS,
        cost_estimate=cost(rows, depth, cols, share),
    )(jnp.stack([first for _, first in up]).astype(jnp.int32), low, owners, acc, *[p for p, _ in up])


ACROSS = [(0, 2), (2, 0), (1, 3), (3, 1)]
SWAP = [(0, 1), (1, 0)]
BESIDE = [(0, 1), (1, 0), (2, 3), (3, 2)]


def half_of(rows, which):
    half = rows.shape[0] // 2
    return lax.dynamic_slice_in_dim(rows, which * half, half, 0)


def shrink_kernel(count, rank, first, *refs):
    piece, xs, owners = refs[0], refs[1:3], refs[3:5]
    before, outs = refs[5:-2], refs[-2:]
    for i in range(2):
        full = lax.dot_general(
            xs[i][...], piece[...], (((1,), (1,)), ((), ())), preferred_element_type=jnp.float32
        )
        kept = jnp.where(owner_mask(owners[i][...], first[0], count, rank), full, 0.0)
        total = jnp.dot(
            kept.astype(jnp.bfloat16), rank_spread(count, rank), preferred_element_type=jnp.float32
        )
        outs[i][...] = total + before[i][...] if before else total


def add_shrunk(lows, piece, first, xs, owners, rank):
    rows, features = xs[0].shape
    whole = pl.BlockSpec(memory_space=pltpu.VMEM)
    args = [piece, *xs, *owners, *lows]
    return pl.pallas_call(
        functools.partial(shrink_kernel, piece.shape[0] // rank, rank),
        in_specs=[pl.BlockSpec(memory_space=pltpu.SMEM)] + [whole] * len(args),
        out_specs=[whole] * 2,
        out_shape=[jax.ShapeDtypeStruct((rows, rank), jnp.float32)] * 2,
        compiler_params=PARAMS,
        cost_estimate=cost(2 * rows, features, piece.shape[0], SHRINK),
    )(first.astype(jnp.int32).reshape(1), *args)


def local_line(requests, query_weight, adapter_down_factor, adapter_up_factor, owners):
    features = requests.shape[1]
    rank = adapter_down_factor.shape[1]
    z = lax.axis_index("tensor")
    inner = (z == 1) | (z == 2)

    me = lax.axis_index("adapter")
    replica = lax.axis_index("replica")
    resident = adapter_down_factor.shape[0]
    down = adapter_down_factor.reshape(resident * rank, features)
    up = adapter_up_factor.reshape(resident * rank, -1)

    pair, middle = [(0, 1), (1, 0), (2, 3), (3, 2)], [(1, 2), (2, 1)]
    second, third = jnp.where(inner, z ^ 3, z ^ 2), jnp.where(inner, z ^ 2, z ^ 3)
    halves = [me * resident, (me ^ 2) * resident + replica * (resident // 2)]
    halves.append((me ^ 2) * resident + (1 - replica) * (resident // 2))

    a1 = lax.ppermute(requests, "tensor", pair)
    m1 = lax.ppermute(requests, "tensor", middle)
    acc = add_block(None, [[requests]], query_weight, z, share=FIRST)
    xs = (requests, lax.ppermute(requests, "adapter", BESIDE))
    both = (owners, lax.ppermute(owners, "adapter", BESIDE))
    down_mine = lax.ppermute(half_of(down, replica), "adapter", ACROSS)
    up_half, up_near = half_of(up, replica), lax.ppermute(up, "adapter", BESIDE)
    lows = add_shrunk((), down, halves[0], xs, both, rank)
    down_mine, acc, lows, up_half, up_near = lax.optimization_barrier(
        (down_mine, acc, lows, up_half, up_near)
    )
    up_mine = lax.ppermute(up_half, "adapter", ACROSS)
    down_other = lax.ppermute(down_mine, "replica", SWAP)
    a1, down_mine = lax.optimization_barrier((a1, down_mine))
    lows = add_shrunk(lows, down_mine, halves[1], xs, both, rank)
    m2 = lax.ppermute(a1, "tensor", middle)
    e2 = lax.ppermute(m1, "tensor", pair)
    acc = add_block(acc, [[a1]], query_weight, z ^ 1)
    lows, acc = lax.optimization_barrier((lows, acc))
    lows = add_shrunk(lows, down_other, halves[2], xs, both, rank)
    low = lows[0] + lax.ppermute(lows[1].astype(jnp.bfloat16), "adapter", BESIDE).astype(jnp.float32)
    low = low.T.astype(jnp.bfloat16)
    shares = jnp.broadcast_to(low[None], (4, *low.shape))
    shares = lax.all_to_all(shares, "tensor", 0, 0)
    low = jnp.sum(shares.astype(jnp.float32), axis=0).astype(jnp.bfloat16).T
    m2, e2, low = lax.optimization_barrier((m2, e2, low))
    e3 = lax.ppermute(m2, "tensor", pair)

    up_other = lax.ppermute(up_mine, "replica", SWAP)
    up_other, _ = lax.optimization_barrier((up_other, m2))
    near = [up_near, *[lax.ppermute(piece, "adapter", BESIDE) for piece in (up_mine, up_other)]]
    across = resident - 2 * (me % 2) * resident
    ups = list(zip((up, up_mine, up_other), halves)) + list(zip(near, [h + across for h in halves]))

    acc = add_block(acc, [[m1, e2]], query_weight, second, inner.astype(jnp.int32))
    weight = lax.dynamic_slice_in_dim(query_weight, third * features, features, 0)
    acc, weight = lax.optimization_barrier((acc, weight))
    acc = add_expanded(acc, low, owners, ups)
    return add_last(acc, inner, m2, e3, weight)


def local_any(requests, query_weight, adapter_down_factor, adapter_up_factor, owners):
    rank, width = adapter_down_factor.shape[1:]
    down, up = (
        lax.all_gather(f, "adapter", axis=0, tiled=True).reshape(-1, width)
        for f in (adapter_down_factor, adapter_up_factor)
    )
    count = down.shape[0] // rank
    full = lax.dot_general(
        requests, down, (((1,), (1,)), ((), ())), preferred_element_type=jnp.float32
    )
    kept = jnp.where(owner_mask(owners, 0, count, rank), full, 0.0).astype(jnp.bfloat16)
    low = jnp.dot(kept, rank_spread(count, rank), preferred_element_type=jnp.float32)
    low = lax.psum(low.astype(jnp.bfloat16), "tensor")
    spread = lax.dot_general(
        low, rank_spread(count, rank), (((1,), (1,)), ((), ())), preferred_element_type=jnp.float32
    )
    kept = jnp.where(owner_mask(owners, 0, count, rank), spread, 0.0).astype(jnp.bfloat16)
    base = jnp.dot(
        lax.all_gather(requests, "tensor", axis=1, tiled=True),
        query_weight,
        preferred_element_type=jnp.float32,
    )
    delta = jnp.dot(kept, up, preferred_element_type=jnp.float32)
    return (base + adapter_scale * delta).astype(jnp.bfloat16)


def solution(mesh):
    placed = (
        P(("replica", "adapter"), "tensor"),
        P(None, "tensor"),
        P("adapter", None, "tensor"),
        P("adapter", None, "tensor"),
        P(("replica", "adapter"), None),
    )
    sizes = tuple(mesh.shape[axis] for axis in ("replica", "tensor", "adapter"))
    return jax.shard_map(
        local_line if sizes == (2, 4, 4) else local_any,
        mesh=mesh,
        in_specs=placed,
        out_specs=P(("replica", "adapter"), "tensor"),
        check_vma=False,
    )
```
